128 devices in a mesh: clip: 4 (over y), seq: 32 (over x, z, core).
Axes of the slice: x: 4, y: 4, z: 4, core: 2. Of those that a mesh axis runs over, the one named last changes fastest.
Arguments:
- tokens: bfloat16 [327680, 1280], P(('clip', 'seq')), parts along dimension 0, may hold values from -6 to 6
- slot_proj: bfloat16 [1280, 64], replicated, may hold values from -5 to 5, as said below
- w_in: bfloat16 [32, 1280, 2560], P('seq'), may hold values from -0.15625 to 0.15625
- w_out: bfloat16 [32, 2560, 1280], P('seq'), may hold values from -0.125 to 0.125
Outputs:
- mixed: bfloat16 [327680, 1280], P(('clip', 'seq')), parts along dimension 0
The draws below stay inside these ranges and needn't reach their ends.
There are 4 independent parts, one for each index of `clip`. The reference program is written for one: setup_inputs(seed, part) draws one part's arguments, and reference() takes and returns one part's arrays. A program takes and returns all parts, laid end to end along the dimension named above; an argument that names none is the same for every part. Nothing has to cross between parts.
Inputs may be any that keep to these rules, and one draw needn't show every extreme that they name: `slot_proj`: the slots' parameters.
All inputs are finite; a program needn't handle non-finite values.
Results may differ from the reference program's by a relative error of at most 0.02.
Values may be sent and summed in bfloat16 or wider, within the bound.
No kernel may reach another device: no remote copies, remote signals or barrier semaphores. Data moves between devices by JAX's collectives and lax.ppermute only.
A program may use at most 64 MiB of HBM per device.

```python
import jax
import jax.numpy as jnp
from jax import lax

D = 1280
FF = 2560
SLOTS = 2
TOKENS = 81920
EXPERTS = 32
SLOTS_ALL = 64


def draw_slot_proj(key, part):
    key = jax.random.fold_in(key, 11)
    base_key, scale_key = jax.random.split(key)
    values = jax.random.truncated_normal(base_key, -4.0, 4.0, (D, SLOTS_ALL), jnp.float32)
    column_scale = jnp.exp(jax.random.uniform(scale_key, (1, SLOTS_ALL), jnp.float32, jnp.log(4.0), jnp.log(16.0)))
    scaled = jnp.clip(values * column_scale / jnp.sqrt(jnp.float32(D)), -5.0, 5.0)
    return scaled.astype(jnp.bfloat16)


def shard_levels(rng, extent, cuts, smallest, top_value):
    factor_of = 1.0
    for axis_at, shards_of in cuts:
        steps = jax.random.uniform(jax.random.fold_in(jax.random.fold_in(rng, 6), axis_at), (shards_of,), jnp.float32, smallest / len(cuts), top_value / len(cuts))
        factor_of = factor_of * jnp.repeat(jnp.exp(steps), extent[axis_at] // shards_of).reshape((-1,) + (1,) * (len(extent) - 1 - axis_at))
    return factor_of


def normal_values(stream_key, shape, spread, most, shards=(), dtype=jnp.bfloat16):
    entries = spread * jax.random.normal(stream_key, shape, jnp.float32)
    if shards:
        entries = entries * shard_levels(stream_key, shape, shards, -0.22, 0.18)
    return jnp.clip(entries, -most, most).astype(dtype)


def setup_inputs(seed: int = 0, part: int = 0) -> dict:
    key_of = jax.random.split(jax.random.key(seed), 5)
    part_keys = jax.random.split(jax.random.fold_in(key_of[4], part), 5)
    return {
        "tokens": normal_values(part_keys[0], (TOKENS, D), 1.0, 6.0, ((0, 32),)),
        "slot_proj": draw_slot_proj(jax.random.fold_in(key_of[4], 71), part),
        "w_in": normal_values(key_of[2], (EXPERTS, D, FF), D ** -0.5, 0.15625, ((0, 32),)),
        "w_out": normal_values(key_of[3], (EXPERTS, FF, D), FF ** -0.5, 0.125, ((0, 32),)),
    }


def run_expert(packed):
    slot_in, first, second = packed
    hidden = jax.nn.gelu(jnp.dot(slot_in, first, preferred_element_type=jnp.float32)).astype(jnp.bfloat16)
    return jnp.dot(hidden, second, preferred_element_type=jnp.float32).astype(jnp.bfloat16)


def reference(tokens, slot_proj, w_in, w_out):
    logits = jnp.dot(tokens, slot_proj, preferred_element_type=jnp.float32)
    col_max = jnp.max(logits, axis=0)
    shifted = jnp.exp(logits - col_max[None, :])
    col_total = jnp.sum(shifted, axis=0)
    dispatch = shifted.astype(jnp.bfloat16)
    slot_num = jnp.dot(dispatch.T, tokens, preferred_element_type=jnp.float32)
    slot_in = (slot_num / col_total[:, None]).astype(jnp.bfloat16)
    slot_in = slot_in.reshape(EXPERTS, SLOTS, D)
    slot_out = lax.map(run_expert, (slot_in, w_in, w_out)).reshape(SLOTS_ALL, D)
    combine = jax.nn.softmax(logits, axis=1).astype(jnp.bfloat16)
    return jnp.dot(combine, slot_out, preferred_element_type=jnp.float32).astype(jnp.bfloat16)
```

```python
import jax
import jax.numpy as jnp
from jax import lax
from jax.sharding import PartitionSpec as P

SLOTS = 2
LANES = 128


def split3(x):
    hi = lax.reduce_precision(x, 8, 7)
    mid = lax.reduce_precision(x - hi, 8, 7)
    return [hi, mid, x - hi - mid]


def body(tokens, slot_proj, w_in, w_out):
    devices = lax.axis_size("seq")
    width = tokens.shape[1]
    logits = jnp.dot(tokens, slot_proj, preferred_element_type=jnp.float32)
    own_max = jnp.max(logits, axis=0)
    shifted = jnp.exp(logits - own_max[None, :])
    own_total = jnp.sum(shifted, axis=0)
    own_num = lax.dot_general(
        shifted.astype(jnp.bfloat16), tokens, (((0,), (0,)), ((), ())), preferred_element_type=jnp.float32
    )
    stats = jnp.stack(split3(own_max) + split3(own_total), axis=1)
    stats = jnp.pad(stats, ((0, 0), (0, LANES - stats.shape[1])))
    sent = jnp.concatenate([own_num, stats], axis=1).astype(jnp.bfloat16)
    got = lax.all_to_all(sent.reshape(devices, -1, width + LANES), "seq", 0, 0).astype(jnp.float32)
    maxes = got[:, :, width] + got[:, :, width + 1] + got[:, :, width + 2]
    totals = got[:, :, width + 3] + got[:, :, width + 4] + got[:, :, width + 5]
    scale = jnp.exp(maxes - jnp.max(maxes, axis=0)[None])
    num = jnp.sum(got[:, :, :width] * scale[:, :, None], axis=0)
    slot_in = (num / jnp.sum(totals * scale, axis=0)[:, None]).astype(jnp.bfloat16)
    slot_in = slot_in.reshape(w_in.shape[0], SLOTS, width)
    hidden = jax.nn.gelu(
        jnp.einsum("esd,edf->esf", slot_in, w_in, preferred_element_type=jnp.float32)
    ).astype(jnp.bfloat16)
    slot_out = jnp.einsum("esf,efd->esd", hidden, w_out, preferred_element_type=jnp.float32).astype(
        jnp.bfloat16
    )
    slot_out = slot_out.reshape(1, -1, width)
    slot_all = lax.all_to_all(jnp.broadcast_to(slot_out, (devices, *slot_out.shape[1:])), "seq", 0, 0)
    combine = jax.nn.softmax(logits, axis=1).astype(jnp.bfloat16)
    mixed = jnp.dot(combine, slot_all.reshape(-1, width), preferred_element_type=jnp.float32)
    return mixed.astype(jnp.bfloat16)


def solution(mesh):
    return jax.shard_map(
        body,
        mesh=mesh,
        in_specs=(P(("clip", "seq"), None), P(), P("seq", None, None), P("seq", None, None)),
        out_specs=P(("clip", "seq"), None),
        check_vma=False,
    )
```

```python
import functools

import jax
import jax.numpy as jnp
from jax import lax
from jax.experimental import pallas as pl
from jax.experimental.pallas import tpu as pltpu
from jax.sharding import PartitionSpec as P

SLOTS = 2
LANES = 128
MIB = 1 << 20
DLIM = 20
OUT = jax.ShapeDtypeStruct


def split3(x):
    hi = x.astype(jnp.bfloat16).astype(jnp.float32)
    mid = (x - hi).astype(jnp.bfloat16).astype(jnp.float32)
    return [hi, mid, x - hi - mid]


def dispatch_kernel(chunks, tokens_ref, proj_hbm, sent_ref, logits_ref, held, acc, proj_ref, sem):
    slots, width = proj_ref.shape
    starts = [sum(chunks[:i]) for i in range(len(chunks))]

    def copy(i):
        part = pl.ds(starts[i], chunks[i])
        return pltpu.make_async_copy(tokens_ref.at[part], held.at[part], sem.at[i])

    proj_copy = pltpu.make_async_copy(proj_hbm, proj_ref, sem.at[len(chunks)])
    proj_copy.start()
    for i in range(len(chunks)):
        copy(i).start()
    proj_copy.wait()

    def halves(i):
        rows = chunks[i] // 2
        return [pl.ds(starts[i] + k * rows, rows) for k in range(2)]

    def chunk_logits(i):
        copy(i).wait()
        blocks = []
        for part in halves(i):
            block = lax.dot_general(
                held[part, :], proj_ref[...], (((1,), (1,)), ((), ())), preferred_element_type=jnp.float32
            )
            logits_ref[part, :] = block
            blocks.append(block)
        return blocks

    top = jnp.full((1, slots), -jnp.inf, jnp.float32)
    total = jnp.zeros((1, slots), jnp.float32)
    blocks = chunk_logits(0)
    for i in range(len(chunks)):
        following = chunk_logits(i + 1) if i + 1 < len(chunks) else None
        new_top = top
        for block in blocks:
            new_top = jnp.maximum(new_top, jnp.max(block, axis=0, keepdims=True))
        fade = jnp.exp(top - new_top)
        total = total * fade
        adds = []
        for part, block in zip(halves(i), blocks):
            shifted = jnp.exp(block - new_top)
            total = total + jnp.sum(shifted, axis=0, keepdims=True)
            adds.append(
                lax.dot_general(
                    shifted.astype(jnp.bfloat16), held[part, :], (((0,), (0,)), ((), ())),
                    preferred_element_type=jnp.float32,
                )
            )
        add = adds[0] + adds[1]
        acc[...] = add if i == 0 else acc[...] * fade.reshape(slots, 1) + add
        top, blocks = new_top, following
    lanes = [*split3(top), *split3(total)]
    stats = jnp.concatenate([*lanes, jnp.zeros((LANES - len(lanes), slots), jnp.float32)], axis=0)
    sums = acc[...].astype(jnp.bfloat16)
    stats = stats.T.astype(jnp.bfloat16)
    for k in range(slots // SLOTS):
        sent_ref[k, :, :width] = sums[SLOTS * k : SLOTS * (k + 1), :]
        sent_ref[k, :, width:] = stats[SLOTS * k : SLOTS * (k + 1), :]


def dispatch(tokens, slot_proj, devices):
    count, width = tokens.shape
    slots = slot_proj.shape[1]
    unit = count // 20
    chunks = (4 * unit, 4 * unit, 6 * unit, 6 * unit)
    return pl.pallas_call(
        functools.partial(dispatch_kernel, chunks),
        out_shape=(
            OUT((devices, slots // devices, width + LANES), jnp.bfloat16),
            OUT((count, slots), jnp.float32),
        ),
        in_specs=[pl.BlockSpec(memory_space=pltpu.HBM)] * 2,
        out_specs=(pl.BlockSpec(memory_space=pltpu.VMEM), pl.BlockSpec(memory_space=pltpu.VMEM)),
        scratch_shapes=[
            pltpu.VMEM((count, width), jnp.bfloat16),
            pltpu.VMEM((slots, width), jnp.float32),
            pltpu.VMEM((slots, width), jnp.bfloat16),
            pltpu.SemaphoreType.DMA((len(chunks) + 1,)),
        ],
        compiler_params=pltpu.CompilerParams(vmem_limit_bytes=DLIM * MIB),
        cost_estimate=pl.CostEstimate(flops=4 * count * width * slots, bytes_accessed=2 * count * width, transcendentals=count * slots),
        name="dispatch",
    )(pltpu.with_memory_space_constraint(tokens, pltpu.HBM), pltpu.with_memory_space_constraint(slot_proj.T, pltpu.HBM))


def combine_kernel(logits_ref, combine_ref):
    block = logits_ref[...]
    shifted = jnp.exp(block - jnp.max(block, axis=1, keepdims=True))
    combine_ref[...] = (shifted / jnp.sum(shifted, axis=1, keepdims=True)).astype(combine_ref.dtype)


def combine_weights(logits):
    return pl.pallas_call(
        combine_kernel,
        out_shape=jax.ShapeDtypeStruct(logits.shape, jnp.bfloat16),
        in_specs=[pl.BlockSpec(memory_space=pltpu.VMEM)],
        out_specs=pl.BlockSpec(memory_space=pltpu.VMEM),
        compiler_params=pltpu.CompilerParams(vmem_limit_bytes=16 * MIB),
        cost_estimate=pl.CostEstimate(flops=5 * logits.size, bytes_accessed=6 * logits.size, transcendentals=logits.size),
        name="combine_weights",
    )(logits)


def expert_kernel(got_ref, w_in_ref, w_out_ref, out_ref, hidden_ref):
    width = w_in_ref.shape[1]
    devices = got_ref.shape[0]
    got = got_ref[...].astype(jnp.float32)
    stats = got[:, :, width:]
    maxes = stats[:, :, 0:1] + stats[:, :, 1:2] + stats[:, :, 2:3]
    totals = stats[:, :, 3:4] + stats[:, :, 4:5] + stats[:, :, 5:6]
    scale = jnp.exp(maxes - jnp.max(maxes, axis=0, keepdims=True))
    num = jnp.sum(got[:, :, :width] * scale, axis=0)
    slot_in = (num / jnp.sum(totals * scale, axis=0)).astype(jnp.bfloat16)
    hidden = jnp.dot(slot_in, w_in_ref[0], preferred_element_type=jnp.float32)
    hidden = jax.nn.gelu(hidden).astype(jnp.bfloat16)
    out = jnp.dot(hidden, w_out_ref[0], preferred_element_type=jnp.float32).astype(jnp.bfloat16)
    for k in range(devices):
        out_ref[k] = out


def expert(got, w_in, w_out):
    devices, slots, _ = got.shape
    return pl.pallas_call(
        expert_kernel,
        out_shape=jax.ShapeDtypeStruct((devices, slots, w_in.shape[1]), jnp.bfloat16),
        in_specs=[pl.BlockSpec(memory_space=pltpu.VMEM)] * 3,
        out_specs=pl.BlockSpec(memory_space=pltpu.VMEM),
        scratch_shapes=[pltpu.VMEM((slots, w_in.shape[2]), jnp.float32)],
        compiler_params=pltpu.CompilerParams(vmem_limit_bytes=WLIM * MIB),
        cost_estimate=pl.CostEstimate(flops=4 * slots * w_in.size, bytes_accessed=4 * w_in.size, transcendentals=slots * w_in.shape[2]),
        name="expert",
    )(got, WC(w_in), WC(w_out))


def mix_kernel(blocks, combine_ref, slot_ref, mixed_ref, slot_all, held, sem):
    rows = combine_ref.shape[0] // blocks
    for k in range(slot_ref.shape[0]):
        slot_all[SLOTS * k : SLOTS * (k + 1), :] = slot_ref[k]
    for i in range(blocks):
        part = pl.ds(i * rows, rows)
        held[part, :] = jnp.dot(
            combine_ref[part, :], slot_all[...], preferred_element_type=jnp.float32
        ).astype(jnp.bfloat16)
        pltpu.make_async_copy(held.at[part], mixed_ref.at[part], sem.at[i]).start()
    for i in range(blocks):
        part = pl.ds(i * rows, rows)
        pltpu.make_async_copy(held.at[part], mixed_ref.at[part], sem.at[i]).wait()


def mix(combine, slot_all, blocks=10):
    count, slots = combine.shape
    width = slot_all.shape[2]
    return pl.pallas_call(
        functools.partial(mix_kernel, blocks),
        out_shape=jax.ShapeDtypeStruct((count, width), jnp.bfloat16),
        in_specs=[pl.BlockSpec(memory_space=pltpu.VMEM)] * 2,
        out_specs=pl.BlockSpec(memory_space=pl.ANY),
        scratch_shapes=[
            pltpu.VMEM((slots, width), jnp.bfloat16),
            pltpu.VMEM((count, width), jnp.bfloat16),
            pltpu.SemaphoreType.DMA((blocks,)),
        ],
        compiler_params=pltpu.CompilerParams(vmem_limit_bytes=24 * MIB),
        cost_estimate=pl.CostEstimate(flops=2 * count * width * slots, bytes_accessed=2 * count * width, transcendentals=0),
        name="mix",
    )(combine, slot_all)


WLIM = 16
def WC(x):
    return pltpu.with_memory_space_constraint(x, pltpu.VMEM)


def body(tokens, slot_proj, w_in, w_out):
    devices = lax.axis_size("seq")
    sent, logits = dispatch(tokens, slot_proj, devices)
    got = lax.all_to_all(sent, "seq", 0, 0)
    combine = combine_weights(logits)
    slot_out = expert(got, w_in, w_out)
    slot_all = lax.all_to_all(slot_out, "seq", 0, 0)
    return mix(combine, slot_all)


def solution(mesh):
    return jax.shard_map(
        body,
        mesh=mesh,
        in_specs=(P(("clip", "seq"), None), P(), P("seq", None, None), P("seq", None, None)),
        out_specs=P(("clip", "seq"), None),
        check_vma=False,
    )
```

```python
import functools

import jax
import jax.numpy as jnp
from jax import lax
from jax.experimental import pallas as pl
from jax.experimental.pallas import tpu as pltpu
from jax.sharding import PartitionSpec as P

SLOTS = 2
LANES = 128
MIB = 1 << 20
DLIM = 20
OUT = jax.ShapeDtypeStruct


def split3(x):
    hi = x.astype(jnp.bfloat16).astype(jnp.float32)
    mid = (x - hi).astype(jnp.bfloat16).astype(jnp.float32)
    return [hi, mid, x - hi - mid]


def dispatch_kernel(chunks, tokens_ref, proj_hbm, sent_ref, logits_ref, held, acc, proj_ref, sem):
    slots, width = proj_ref.shape
    starts = [sum(chunks[:i]) for i in range(len(chunks))]

    def copy(i):
        part = pl.ds(starts[i], chunks[i])
        return pltpu.make_async_copy(tokens_ref.at[part], held.at[part], sem.at[i])

    proj_copy = pltpu.make_async_copy(proj_hbm, proj_ref, sem.at[len(chunks)])
    proj_copy.start()
    for i in range(len(chunks)):
        copy(i).start()
    proj_copy.wait()

    def halves(i):
        rows = chunks[i] // 2
        return [pl.ds(starts[i] + k * rows, rows) for k in range(2)]

    def chunk_logits(i):
        copy(i).wait()
        blocks = []
        for part in halves(i):
            block = lax.dot_general(
                held[part, :], proj_ref[...], (((1,), (1,)), ((), ())), preferred_element_type=jnp.float32
            )
            logits_ref[part, :] = block
            blocks.append(block)
        return blocks

    top = jnp.full((1, slots), -jnp.inf, jnp.float32)
    total = jnp.zeros((1, slots), jnp.float32)
    blocks = chunk_logits(0)
    for i in range(len(chunks)):
        following = chunk_logits(i + 1) if i + 1 < len(chunks) else None
        new_top = top
        for block in blocks:
            new_top = jnp.maximum(new_top, jnp.max(block, axis=0, keepdims=True))
        fade = jnp.exp(top - new_top)
        total = total * fade
        adds = []
        for part, block in zip(halves(i), blocks):
            shifted = jnp.exp(block - new_top)
            total = total + jnp.sum(shifted, axis=0, keepdims=True)
            adds.append(
                lax.dot_general(
                    shifted.astype(jnp.bfloat16), held[part, :], (((0,), (0,)), ((), ())),
                    preferred_element_type=jnp.float32,
                )
            )
        add = adds[0] + adds[1]
        acc[...] = add if i == 0 else acc[...] * fade.reshape(slots, 1) + add
        top, blocks = new_top, following
    lanes = [*split3(top), *split3(total)]
    stats = jnp.concatenate([*lanes, jnp.zeros((LANES - len(lanes), slots), jnp.float32)], axis=0)
    sums = acc[...].astype(jnp.bfloat16)
    stats = stats.T.astype(jnp.bfloat16)
    for k in range(slots // SLOTS):
        sent_ref[k, :, :width] = sums[SLOTS * k : SLOTS * (k + 1), :]
        sent_ref[k, :, width:] = stats[SLOTS * k : SLOTS * (k + 1), :]


def dispatch(tokens, slot_proj, devices):
    count, width = tokens.shape
    slots = slot_proj.shape[1]
    unit = count // 20
    chunks = (4 * unit, 4 * unit, 6 * unit, 6 * unit)
    return pl.pallas_call(
        functools.partial(dispatch_kernel, chunks),
        out_shape=(
            OUT((devices, slots // devices, width + LANES), jnp.bfloat16),
            OUT((count, slots), jnp.float32),
        ),
        in_specs=[pl.BlockSpec(memory_space=pltpu.HBM)] * 2,
        out_specs=(pl.BlockSpec(memory_space=pltpu.VMEM), pl.BlockSpec(memory_space=pltpu.VMEM)),
        scratch_shapes=[
            pltpu.VMEM((count, width), jnp.bfloat16),
            pltpu.VMEM((slots, width), jnp.float32),
            pltpu.VMEM((slots, width), jnp.bfloat16),
            pltpu.SemaphoreType.DMA((len(chunks) + 1,)),
        ],
        compiler_params=pltpu.CompilerParams(vmem_limit_bytes=DLIM * MIB),
        cost_estimate=pl.CostEstimate(flops=32 * count * width * slots, bytes_accessed=2 * count * width, transcendentals=count * slots),
        name="dispatch",
    )(pltpu.with_memory_space_constraint(tokens, pltpu.HBM), pltpu.with_memory_space_constraint(slot_proj.T, pltpu.HBM))


def combine_kernel(logits_ref, combine_ref):
    block = logits_ref[...]
    shifted = jnp.exp(block - jnp.max(block, axis=1, keepdims=True))
    combine_ref[...] = (shifted / jnp.sum(shifted, axis=1, keepdims=True)).astype(combine_ref.dtype)


def combine_weights(logits):
    return pl.pallas_call(
        combine_kernel,
        out_shape=jax.ShapeDtypeStruct(logits.shape, jnp.bfloat16),
        in_specs=[pl.BlockSpec(memory_space=pltpu.VMEM)],
        out_specs=pl.BlockSpec(memory_space=pltpu.VMEM),
        compiler_params=pltpu.CompilerParams(vmem_limit_bytes=16 * MIB),
        cost_estimate=pl.CostEstimate(flops=5 * logits.size, bytes_accessed=6 * logits.size, transcendentals=logits.size),
        name="combine_weights",
    )(logits)


def expert_kernel(got_ref, w_in_ref, w_out_ref, out_ref, hidden_ref):
    width = w_in_ref.shape[1]
    devices = got_ref.shape[0]
    got = got_ref[...].astype(jnp.float32)
    stats = got[:, :, width:]
    maxes = stats[:, :, 0:1] + stats[:, :, 1:2] + stats[:, :, 2:3]
    totals = stats[:, :, 3:4] + stats[:, :, 4:5] + stats[:, :, 5:6]
    scale = jnp.exp(maxes - jnp.max(maxes, axis=0, keepdims=True))
    num = jnp.sum(got[:, :, :width] * scale, axis=0)
    slot_in = (num / jnp.sum(totals * scale, axis=0)).astype(jnp.bfloat16)
    hidden = jnp.dot(slot_in, w_in_ref[0], preferred_element_type=jnp.float32)
    hidden = jax.nn.gelu(hidden).astype(jnp.bfloat16)
    out = jnp.dot(hidden, w_out_ref[0], preferred_element_type=jnp.float32).astype(jnp.bfloat16)
    for k in range(devices):
        out_ref[k] = out


def expert(got, w_in, w_out):
    devices, slots, _ = got.shape
    return pl.pallas_call(
        expert_kernel,
        out_shape=jax.ShapeDtypeStruct((devices, slots, w_in.shape[1]), jnp.bfloat16),
        in_specs=[pl.BlockSpec(memory_space=pltpu.VMEM)] * 3,
        out_specs=pl.BlockSpec(memory_space=pltpu.VMEM),
        scratch_shapes=[pltpu.VMEM((slots, w_in.shape[2]), jnp.float32)],
        compiler_params=pltpu.CompilerParams(vmem_limit_bytes=WLIM * MIB),
        cost_estimate=pl.CostEstimate(flops=4 * slots * w_in.size, bytes_accessed=4 * w_in.size, transcendentals=slots * w_in.shape[2]),
        name="expert",
    )(got, WC(w_in), WC(w_out))


def mix_kernel(blocks, combine_ref, slot_ref, mixed_ref, slot_all, held, sem):
    rows = combine_ref.shape[0] // blocks
    for k in range(slot_ref.shape[0]):
        slot_all[SLOTS * k : SLOTS * (k + 1), :] = slot_ref[k]
    for i in range(blocks):
        part = pl.ds(i * rows, rows)
        held[part, :] = jnp.dot(
            combine_ref[part, :], slot_all[...], preferred_element_type=jnp.float32
        ).astype(jnp.bfloat16)
        pltpu.make_async_copy(held.at[part], mixed_ref.at[part], sem.at[i]).start()
    for i in range(blocks):
        part = pl.ds(i * rows, rows)
        pltpu.make_async_copy(held.at[part], mixed_ref.at[part], sem.at[i]).wait()


def mix(combine, slot_all, blocks=10):
    count, slots = combine.shape
    width = slot_all.shape[2]
    return pl.pallas_call(
        functools.partial(mix_kernel, blocks),
        out_shape=jax.ShapeDtypeStruct((count, width), jnp.bfloat16),
        in_specs=[pl.BlockSpec(memory_space=pltpu.VMEM)] * 2,
        out_specs=pl.BlockSpec(memory_space=pl.ANY),
        scratch_shapes=[
            pltpu.VMEM((slots, width), jnp.bfloat16),
            pltpu.VMEM((count, width), jnp.bfloat16),
            pltpu.SemaphoreType.DMA((blocks,)),
        ],
        compiler_params=pltpu.CompilerParams(vmem_limit_bytes=24 * MIB),
        cost_estimate=pl.CostEstimate(flops=2 * count * width * slots, bytes_accessed=2 * count * width, transcendentals=0),
        name="mix",
    )(combine, slot_all)


WLIM = 16
def WC(x):
    return pltpu.with_memory_space_constraint(x, pltpu.VMEM)


def body(tokens, slot_proj, w_in, w_out):
    devices = lax.axis_size("seq")
    sent, logits = dispatch(tokens, slot_proj, devices)
    got = lax.all_to_all(sent, "seq", 0, 0)
    combine = combine_weights(logits)
    slot_out = expert(got, w_in, w_out)
    slot_all = lax.all_to_all(slot_out, "seq", 0, 0)
    return mix(combine, slot_all)


def solution(mesh):
    return jax.shard_map(
        body,
        mesh=mesh,
        in_specs=(P(("clip", "seq"), None), P(), P("seq", None, None), P("seq", None, None)),
        out_specs=P(("clip", "seq"), None),
        check_vma=False,
    )
```

```python
import functools

import jax
import jax.numpy as jnp
from jax import lax
from jax.experimental import pallas as pl
from jax.experimental.pallas import tpu as pltpu
from jax.sharding import PartitionSpec as P

SLOTS = 2
LANES = 128
MIB = 1 << 20
ORDER1 = [31, 30, 29, 28, 27, 26, 25, 24, 23, 22, 21, 20, 19, 18, 17, 16, 15, 14, 13, 12, 11, 10, 9, 8, 7, 6, 5, 4, 3, 2, 1, 0]
ORDER2 = [21, 20, 29, 28, 23, 22, 19, 18, 13, 12, 31, 30, 27, 26, 17, 16, 15, 14, 11, 10, 5, 4, 25, 24, 9, 8, 7, 6, 3, 2, 1, 0]
DLIM = 20
OUT = jax.ShapeDtypeStruct


def split3(x):
    hi = x.astype(jnp.bfloat16).astype(jnp.float32)
    mid = (x - hi).astype(jnp.bfloat16).astype(jnp.float32)
    return [hi, mid, x - hi - mid]


def dispatch_kernel(chunks, tokens_ref, proj_hbm, sent_ref, logits_ref, held, acc, proj_ref, sem):
    slots, width = proj_ref.shape
    starts = [sum(chunks[:i]) for i in range(len(chunks))]

    def copy(i):
        part = pl.ds(starts[i], chunks[i])
        return pltpu.make_async_copy(tokens_ref.at[part], held.at[part], sem.at[i])

    proj_copy = pltpu.make_async_copy(proj_hbm, proj_ref, sem.at[len(chunks)])
    proj_copy.start()
    for i in range(len(chunks)):
        copy(i).start()
    proj_copy.wait()

    def halves(i):
        rows = chunks[i] // 2
        return [pl.ds(starts[i] + k * rows, rows) for k in range(2)]

    def chunk_logits(i):
        copy(i).wait()
        blocks = []
        for part in halves(i):
            block = lax.dot_general(
                held[part, :], proj_ref[...], (((1,), (1,)), ((), ())), preferred_element_type=jnp.float32
            )
            logits_ref[part, :] = block
            blocks.append(block)
        return blocks

    top = jnp.full((1, slots), -jnp.inf, jnp.float32)
    total = jnp.zeros((1, slots), jnp.float32)
    blocks = chunk_logits(0)
    for i in range(len(chunks)):
        following = chunk_logits(i + 1) if i + 1 < len(chunks) else None
        new_top = top
        for block in blocks:
            new_top = jnp.maximum(new_top, jnp.max(block, axis=0, keepdims=True))
        fade = jnp.exp(top - new_top)
        total = total * fade
        adds = []
        for part, block in zip(halves(i), blocks):
            shifted = jnp.exp(block - new_top)
            total = total + jnp.sum(shifted, axis=0, keepdims=True)
            adds.append(
                lax.dot_general(
                    shifted.astype(jnp.bfloat16), held[part, :], (((0,), (0,)), ((), ())),
                    preferred_element_type=jnp.float32,
                )
            )
        add = adds[0] + adds[1]
        acc[...] = add if i == 0 else acc[...] * fade.reshape(slots, 1) + add
        top, blocks = new_top, following
    lanes = [*split3(top), *split3(total)]
    stats = jnp.concatenate([*lanes, jnp.zeros((LANES - len(lanes), slots), jnp.float32)], axis=0)
    sums = acc[...].astype(jnp.bfloat16)
    stats = stats.T.astype(jnp.bfloat16)
    for j in range(slots // SLOTS):
        k = ORDER1[j]
        sent_ref[j, :, :width] = sums[SLOTS * k : SLOTS * (k + 1), :]
        sent_ref[j, :, width:] = stats[SLOTS * k : SLOTS * (k + 1), :]


def dispatch(tokens, slot_proj, devices):
    count, width = tokens.shape
    slots = slot_proj.shape[1]
    unit = count // 20
    chunks = (4 * unit, 4 * unit, 6 * unit, 6 * unit)
    return pl.pallas_call(
        functools.partial(dispatch_kernel, chunks),
        out_shape=(
            OUT((devices, slots // devices, width + LANES), jnp.bfloat16),
            OUT((count, slots), jnp.float32),
        ),
        in_specs=[pl.BlockSpec(memory_space=pltpu.HBM)] * 2,
        out_specs=(pl.BlockSpec(memory_space=pltpu.VMEM), pl.BlockSpec(memory_space=pltpu.VMEM)),
        scratch_shapes=[
            pltpu.VMEM((count, width), jnp.bfloat16),
            pltpu.VMEM((slots, width), jnp.float32),
            pltpu.VMEM((slots, width), jnp.bfloat16),
            pltpu.SemaphoreType.DMA((len(chunks) + 1,)),
        ],
        compiler_params=pltpu.CompilerParams(vmem_limit_bytes=DLIM * MIB),
        cost_estimate=pl.CostEstimate(flops=32 * count * width * slots, bytes_accessed=2 * count * width, transcendentals=count * slots),
        name="dispatch",
    )(pltpu.with_memory_space_constraint(tokens, pltpu.HBM), pltpu.with_memory_space_constraint(slot_proj.T, pltpu.HBM))


def halves_dot(rows, weights_ref):
    half = weights_ref.shape[2] // 2
    return [
        jnp.dot(rows, weights_ref[0, :, k * half : (k + 1) * half], preferred_element_type=jnp.float32) for k in range(2)
    ]


def expert_kernel(got_ref, w_in_ref, w_out_ref, out_ref):
    width = w_in_ref.shape[1]
    devices = got_ref.shape[0]
    got = got_ref[...].astype(jnp.float32)
    stats = got[:, :, width:]
    maxes = stats[:, :, 0:1] + stats[:, :, 1:2] + stats[:, :, 2:3]
    totals = stats[:, :, 3:4] + stats[:, :, 4:5] + stats[:, :, 5:6]
    scale = jnp.exp(maxes - jnp.max(maxes, axis=0, keepdims=True))
    num = jnp.sum(got[:, :, :width] * scale, axis=0)
    slot_in = (num / jnp.sum(totals * scale, axis=0)).astype(jnp.bfloat16)
    hidden = jnp.concatenate([jax.nn.gelu(h).astype(jnp.bfloat16) for h in halves_dot(slot_in, w_in_ref)], axis=1)
    out = jnp.concatenate([o.astype(jnp.bfloat16) for o in halves_dot(hidden, w_out_ref)], axis=1)
    for k in range(devices):
        out_ref[k] = out


def expert(got, w_in, w_out):
    devices, slots, _ = got.shape
    return pl.pallas_call(
        expert_kernel,
        out_shape=jax.ShapeDtypeStruct((devices, slots, w_in.shape[1]), jnp.bfloat16),
        in_specs=[pl.BlockSpec(memory_space=pltpu.VMEM)] * 3,
        out_specs=pl.BlockSpec(memory_space=pltpu.VMEM),
        compiler_params=pltpu.CompilerParams(vmem_limit_bytes=WLIM * MIB),
        cost_estimate=pl.CostEstimate(flops=4 * slots * w_in.size, bytes_accessed=4 * w_in.size, transcendentals=slots * w_in.shape[2]),
        name="expert",
    )(got, WC(w_in), WC(w_out))


def mix_kernel(chunks, logits_ref, slot_ref, mixed_ref, slot_all, held, sem):
    for k in range(slot_ref.shape[0]):
        slot_all[SLOTS * ORDER2[k] : SLOTS * (ORDER2[k] + 1), :] = slot_ref[k]
    starts = [sum(chunks[:i]) for i in range(len(chunks))]

    def copy(i):
        part = pl.ds(starts[i], chunks[i])
        return pltpu.make_async_copy(held.at[part], mixed_ref.at[part], sem.at[i])

    for i in range(len(chunks)):
        rows = chunks[i] // 2
        for part in [pl.ds(starts[i] + k * rows, rows) for k in range(2)]:
            block = logits_ref[part, :]
            shifted = jnp.exp(block - jnp.max(block, axis=1, keepdims=True))
            combine = (shifted / jnp.sum(shifted, axis=1, keepdims=True)).astype(jnp.bfloat16)
            held[part, :] = jnp.dot(combine, slot_all[...], preferred_element_type=jnp.float32).astype(jnp.bfloat16)
        copy(i).start()
    for i in range(len(chunks)):
        copy(i).wait()


def mix(logits, slot_all):
    count, slots = logits.shape
    width = slot_all.shape[2]
    chunks = (count // 10,) * 10
    return pl.pallas_call(
        functools.partial(mix_kernel, chunks),
        out_shape=jax.ShapeDtypeStruct((count, width), jnp.bfloat16),
        in_specs=[pl.BlockSpec(memory_space=pltpu.VMEM)] * 2,
        out_specs=pl.BlockSpec(memory_space=pl.ANY),
        scratch_shapes=[
            pltpu.VMEM((slots, width), jnp.bfloat16),
            pltpu.VMEM((count, width), jnp.bfloat16),
            pltpu.SemaphoreType.DMA((len(chunks),)),
        ],
        compiler_params=pltpu.CompilerParams(vmem_limit_bytes=24 * MIB),
        cost_estimate=pl.CostEstimate(flops=2 * count * width * slots, bytes_accessed=2 * count * width, transcendentals=count * slots),
        name="mix",
    )(logits, slot_all)


WLIM = 16
def WC(x):
    return pltpu.with_memory_space_constraint(x, pltpu.VMEM)


def body(tokens, slot_proj, w_in, w_out):
    devices = lax.axis_size("seq")
    sent, logits = dispatch(tokens, slot_proj, devices)
    got = lax.all_to_all(sent, "seq", 0, 0, axis_index_groups=[list(ORDER1)])
    slot_out = expert(got, w_in, w_out)
    slot_all = lax.all_to_all(slot_out, "seq", 0, 0, axis_index_groups=[list(ORDER2)])
    return mix(logits, slot_all)


def solution(mesh):
    return jax.shard_map(
        body,
        mesh=mesh,
        in_specs=(P(("clip", "seq"), None), P(), P("seq", None, None), P("seq", None, None)),
        out_specs=P(("clip", "seq"), None),
        check_vma=False,
    )
```

```python
import functools

import jax
import jax.numpy as jnp
from jax import lax
from jax.experimental import pallas as pl
from jax.experimental.pallas import tpu as pltpu
from jax.sharding import PartitionSpec as P

SLOTS = 2
LANES = 128
MIB = 1 << 20
ORDER1 = [23, 22, 21, 20, 19, 18, 17, 16, 15, 14, 13, 12, 11, 10, 9, 8, 7, 6, 5, 4, 3, 2, 1, 0, 31, 30, 29, 28, 27, 26, 25, 24]
ORDER2 = [21, 20, 29, 28, 23, 22, 19, 18, 13, 12, 31, 30, 27, 26, 17, 16, 15, 14, 11, 10, 5, 4, 25, 24, 9, 8, 7, 6, 3, 2, 1, 0]
DLIM = 20
OUT = jax.ShapeDtypeStruct


def split3(x):
    hi = x.astype(jnp.bfloat16).astype(jnp.float32)
    mid = (x - hi).astype(jnp.bfloat16).astype(jnp.float32)
    return [hi, mid, x - hi - mid]


def dispatch_kernel(chunks, tokens_ref, proj_hbm, sent_ref, logits_ref, held, acc, proj_ref, sem):
    slots, width = proj_ref.shape
    starts = [sum(chunks[:i]) for i in range(len(chunks))]

    def copy(i):
        part = pl.ds(starts[i], chunks[i])
        return pltpu.make_async_copy(tokens_ref.at[part], held.at[part], sem.at[i])

    proj_copy = pltpu.make_async_copy(proj_hbm, proj_ref, sem.at[len(chunks)])
    proj_copy.start()
    for i in range(len(chunks)):
        copy(i).start()
    proj_copy.wait()

    def halves(i):
        rows = chunks[i] // 2
        return [pl.ds(starts[i] + k * rows, rows) for k in range(2)]

    def chunk_logits(i):
        copy(i).wait()
        blocks = []
        for part in halves(i):
            block = lax.dot_general(
                held[part, :], proj_ref[...], (((1,), (1,)), ((), ())), preferred_element_type=jnp.float32
            )
            logits_ref[part, :] = block
            blocks.append(block)
        return blocks

    top = jnp.full((1, slots), -jnp.inf, jnp.float32)
    total = jnp.zeros((1, slots), jnp.float32)
    blocks = chunk_logits(0)
    for i in range(len(chunks)):
        following = chunk_logits(i + 1) if i + 1 < len(chunks) else None
        new_top = top
        for block in blocks:
            new_top = jnp.maximum(new_top, jnp.max(block, axis=0, keepdims=True))
        fade = jnp.exp(top - new_top)
        total = total * fade
        adds = []
        for part, block in zip(halves(i), blocks):
            shifted = jnp.exp(block - new_top)
            total = total + jnp.sum(shifted, axis=0, keepdims=True)
            adds.append(
                lax.dot_general(
                    shifted.astype(jnp.bfloat16), held[part, :], (((0,), (0,)), ((), ())),
                    preferred_element_type=jnp.float32,
                )
            )
        add = adds[0] + adds[1]
        acc[...] = add if i == 0 else acc[...] * fade.reshape(slots, 1) + add
        top, blocks = new_top, following
    lanes = [*split3(top), *split3(total)]
    stats = jnp.concatenate([*lanes, jnp.zeros((LANES - len(lanes), slots), jnp.float32)], axis=0)
    sums = acc[...].astype(jnp.bfloat16)
    stats = stats.T.astype(jnp.bfloat16)
    for j in range(slots // SLOTS):
        k = ORDER1[j]
        sent_ref[j, :, :width] = sums[SLOTS * k : SLOTS * (k + 1), :]
        sent_ref[j, :, width:] = stats[SLOTS * k : SLOTS * (k + 1), :]


def dispatch(tokens, slot_proj, devices):
    count, width = tokens.shape
    slots = slot_proj.shape[1]
    unit = count // 20
    chunks = (4 * unit, 4 * unit, 6 * unit, 6 * unit)
    return pl.pallas_call(
        functools.partial(dispatch_kernel, chunks),
        out_shape=(
            OUT((devices, slots // devices, width + LANES), jnp.bfloat16),
            OUT((count, slots), jnp.float32),
        ),
        in_specs=[pl.BlockSpec(memory_space=pltpu.HBM)] * 2,
        out_specs=(pl.BlockSpec(memory_space=pltpu.VMEM), pl.BlockSpec(memory_space=pltpu.VMEM)),
        scratch_shapes=[
            pltpu.VMEM((count, width), jnp.bfloat16),
            pltpu.VMEM((slots, width), jnp.float32),
            pltpu.VMEM((slots, width), jnp.bfloat16),
            pltpu.SemaphoreType.DMA((len(chunks) + 1,)),
        ],
        compiler_params=pltpu.CompilerParams(vmem_limit_bytes=DLIM * MIB),
        cost_estimate=pl.CostEstimate(flops=32 * count * width * slots, bytes_accessed=2 * count * width, transcendentals=count * slots),
        name="dispatch",
    )(pltpu.with_memory_space_constraint(tokens, pltpu.HBM), pltpu.with_memory_space_constraint(slot_proj.T, pltpu.HBM))


def halves_dot(rows, weights_ref):
    half = weights_ref.shape[2] // 2
    return [
        jnp.dot(rows, weights_ref[0, :, k * half : (k + 1) * half], preferred_element_type=jnp.float32) for k in range(2)
    ]


def expert_kernel(got_ref, w_in_ref, w_out_ref, out_ref):
    width = w_in_ref.shape[1]
    devices = got_ref.shape[0]
    got = got_ref[...].astype(jnp.float32)
    stats = got[:, :, width:]
    maxes = stats[:, :, 0:1] + stats[:, :, 1:2] + stats[:, :, 2:3]
    totals = stats[:, :, 3:4] + stats[:, :, 4:5] + stats[:, :, 5:6]
    scale = jnp.exp(maxes - jnp.max(maxes, axis=0, keepdims=True))
    num = jnp.sum(got[:, :, :width] * scale, axis=0)
    slot_in = (num / jnp.sum(totals * scale, axis=0)).astype(jnp.bfloat16)
    hidden = jnp.concatenate([jax.nn.gelu(h).astype(jnp.bfloat16) for h in halves_dot(slot_in, w_in_ref)], axis=1)
    out = jnp.concatenate([o.astype(jnp.bfloat16) for o in halves_dot(hidden, w_out_ref)], axis=1)
    for k in range(devices):
        out_ref[k] = out


def expert(got, w_in, w_out):
    devices, slots, _ = got.shape
    return pl.pallas_call(
        expert_kernel,
        out_shape=jax.ShapeDtypeStruct((devices, slots, w_in.shape[1]), jnp.bfloat16),
        in_specs=[pl.BlockSpec(memory_space=pltpu.VMEM)] * 3,
        out_specs=pl.BlockSpec(memory_space=pltpu.VMEM),
        compiler_params=pltpu.CompilerParams(vmem_limit_bytes=WLIM * MIB),
        cost_estimate=pl.CostEstimate(flops=4 * slots * w_in.size, bytes_accessed=4 * w_in.size, transcendentals=slots * w_in.shape[2]),
        name="expert",
    )(got, WC(w_in), WC(w_out))


def mix_kernel(chunks, logits_ref, slot_ref, mixed_ref, slot_all, held, sem):
    for k in range(slot_ref.shape[0]):
        slot_all[SLOTS * ORDER2[k] : SLOTS * (ORDER2[k] + 1), :] = slot_ref[k]
    starts = [sum(chunks[:i]) for i in range(len(chunks))]

    def copy(i):
        part = pl.ds(starts[i], chunks[i])
        return pltpu.make_async_copy(held.at[part], mixed_ref.at[part], sem.at[i])

    for i in range(len(chunks)):
        rows = chunks[i] // 2
        for part in [pl.ds(starts[i] + k * rows, rows) for k in range(2)]:
            block = logits_ref[part, :]
            shifted = jnp.exp(block - jnp.max(block, axis=1, keepdims=True))
            combine = (shifted / jnp.sum(shifted, axis=1, keepdims=True)).astype(jnp.bfloat16)
            held[part, :] = jnp.dot(combine, slot_all[...], preferred_element_type=jnp.float32).astype(jnp.bfloat16)
        copy(i).start()
    for i in range(len(chunks)):
        copy(i).wait()


def mix(logits, slot_all):
    count, slots = logits.shape
    width = slot_all.shape[2]
    chunks = (count // 10,) * 10
    return pl.pallas_call(
        functools.partial(mix_kernel, chunks),
        out_shape=jax.ShapeDtypeStruct((count, width), jnp.bfloat16),
        in_specs=[pl.BlockSpec(memory_space=pltpu.VMEM)] * 2,
        out_specs=pl.BlockSpec(memory_space=pl.ANY),
        scratch_shapes=[
            pltpu.VMEM((slots, width), jnp.bfloat16),
            pltpu.VMEM((count, width), jnp.bfloat16),
            pltpu.SemaphoreType.DMA((len(chunks),)),
        ],
        compiler_params=pltpu.CompilerParams(vmem_limit_bytes=24 * MIB),
        cost_estimate=pl.CostEstimate(flops=2 * count * width * slots, bytes_accessed=2 * count * width, transcendentals=count * slots),
        name="mix",
    )(logits, slot_all)


WLIM = 16
def WC(x):
    return pltpu.with_memory_space_constraint(x, pltpu.VMEM)


def body(tokens, slot_proj, w_in, w_out):
    devices = lax.axis_size("seq")
    sent, logits = dispatch(tokens, slot_proj, devices)
    got = lax.all_to_all(sent, "seq", 0, 0, axis_index_groups=[list(ORDER1)])
    slot_out = expert(got, w_in, w_out)
    slot_all = lax.all_to_all(slot_out, "seq", 0, 0, axis_index_groups=[list(ORDER2)])
    return mix(logits, slot_all)


def solution(mesh):
    return jax.shard_map(
        body,
        mesh=mesh,
        in_specs=(P(("clip", "seq"), None), P(), P("seq", None, None), P("seq", None, None)),
        out_specs=P(("clip", "seq"), None),
        check_vma=False,
    )
```

```python
import functools

import jax
import jax.numpy as jnp
from jax import lax
from jax.experimental import pallas as pl
from jax.experimental.pallas import tpu as pltpu
from jax.sharding import PartitionSpec as P

SLOTS = 2
LANES = 128
MIB = 1 << 20
SIDE = 4


def steps_from_origin(index):
    x, z = index // (2 * SIDE), index // 2 % SIDE
    return min(x, SIDE - x) + min(z, SIDE - z)


ORDER1 = [(23 - i) % 32 for i in range(32)]
ORDER2 = sorted(range(32), key=lambda i: (steps_from_origin(i), i), reverse=True)


def split3(x):
    hi = x.astype(jnp.bfloat16).astype(jnp.float32)
    mid = (x - hi).astype(jnp.bfloat16).astype(jnp.float32)
    return [hi, mid, x - hi - mid]


def dispatch_kernel(chunks, tokens_ref, proj_hbm, sent_ref, logits_ref, held, acc, proj_ref, sem):
    slots, width = proj_ref.shape
    starts = [sum(chunks[:i]) for i in range(len(chunks))]

    def copy(i):
        part = pl.ds(starts[i], chunks[i])
        return pltpu.make_async_copy(tokens_ref.at[part], held.at[part], sem.at[i])

    proj_copy = pltpu.make_async_copy(proj_hbm, proj_ref, sem.at[len(chunks)])
    proj_copy.start()
    for i in range(len(chunks)):
        copy(i).start()
    proj_copy.wait()

    def halves(i):
        rows = chunks[i] // 2
        return [pl.ds(starts[i] + k * rows, rows) for k in range(2)]

    def chunk_logits(i):
        copy(i).wait()
        blocks = []
        for part in halves(i):
            block = lax.dot_general(
                held[part, :], proj_ref[...], (((1,), (1,)), ((), ())), preferred_element_type=jnp.float32
            )
            logits_ref[part, :] = block
            blocks.append(block)
        return blocks

    top = jnp.full((1, slots), -jnp.inf, jnp.float32)
    total = jnp.zeros((1, slots), jnp.float32)
    blocks = chunk_logits(0)
    for i in range(len(chunks)):
        following = chunk_logits(i + 1) if i + 1 < len(chunks) else None
        new_top = top
        for block in blocks:
            new_top = jnp.maximum(new_top, jnp.max(block, axis=0, keepdims=True))
        fade = jnp.exp(top - new_top)
        total = total * fade
        adds = []
        for part, block in zip(halves(i), blocks):
            shifted = jnp.exp(block - new_top)
            total = total + jnp.sum(shifted, axis=0, keepdims=True)
            adds.append(
                lax.dot_general(
                    shifted.astype(jnp.bfloat16), held[part, :], (((0,), (0,)), ((), ())),
                    preferred_element_type=jnp.float32,
                )
            )
        add = adds[0] + adds[1]
        acc[...] = add if i == 0 else acc[...] * fade.reshape(slots, 1) + add
        top, blocks = new_top, following
    lanes = [*split3(top), *split3(total)]
    stats = jnp.concatenate([*lanes, jnp.zeros((LANES - len(lanes), slots), jnp.float32)], axis=0)
    sums = acc[...].astype(jnp.bfloat16)
    stats = stats.T.astype(jnp.bfloat16)
    for j in range(slots // SLOTS):
        k = ORDER1[j]
        sent_ref[j, :, :width] = sums[SLOTS * k : SLOTS * (k + 1), :]
        sent_ref[j, :, width:] = stats[SLOTS * k : SLOTS * (k + 1), :]


def dispatch(tokens, slot_proj, devices):
    count, width = tokens.shape
    slots = slot_proj.shape[1]
    unit = count // 20
    chunks = (4 * unit, 4 * unit, 6 * unit, 6 * unit)
    return pl.pallas_call(
        functools.partial(dispatch_kernel, chunks),
        out_shape=(
            jax.ShapeDtypeStruct((devices, slots // devices, width + LANES), jnp.bfloat16),
            jax.ShapeDtypeStruct((count, slots), jnp.float32),
        ),
        in_specs=[pl.BlockSpec(memory_space=pltpu.HBM)] * 2,
        out_specs=(pl.BlockSpec(memory_space=pltpu.VMEM), pl.BlockSpec(memory_space=pltpu.VMEM)),
        scratch_shapes=[
            pltpu.VMEM((count, width), jnp.bfloat16),
            pltpu.VMEM((slots, width), jnp.float32),
            pltpu.VMEM((slots, width), jnp.bfloat16),
            pltpu.SemaphoreType.DMA((len(chunks) + 1,)),
        ],
        compiler_params=pltpu.CompilerParams(vmem_limit_bytes=20 * MIB),
        cost_estimate=pl.CostEstimate(
            flops=32 * count * width * slots, bytes_accessed=2 * count * width, transcendentals=count * slots
        ),
        name="dispatch",
    )(pltpu.with_memory_space_constraint(tokens, pltpu.HBM), pltpu.with_memory_space_constraint(slot_proj.T, pltpu.HBM))


def halves_dot(rows, weights_ref):
    half = weights_ref.shape[2] // 2
    return [
        jnp.dot(rows, weights_ref[0, :, k * half : (k + 1) * half], preferred_element_type=jnp.float32) for k in range(2)
    ]


def expert_kernel(got_ref, w_in_ref, w_out_ref, out_ref):
    width = w_in_ref.shape[1]
    devices = got_ref.shape[0]
    stats = got_ref[:, :, width:].astype(jnp.float32)
    maxes = stats[:, :, 0:1] + stats[:, :, 1:2] + stats[:, :, 2:3]
    totals = stats[:, :, 3:4] + stats[:, :, 4:5] + stats[:, :, 5:6]
    scale = jnp.exp(maxes - jnp.max(maxes, axis=0, keepdims=True))
    terms = [got_ref[k, :, :width].astype(jnp.float32) * scale[k] for k in range(devices)]
    while len(terms) > 4:
        terms = [sum(terms[k + 4 :: 4], terms[k]) for k in range(4)]
    num = (terms[0] + terms[1]) + (terms[2] + terms[3])
    slot_in = (num / jnp.sum(totals * scale, axis=0)).astype(jnp.bfloat16)
    hidden = jnp.concatenate([jax.nn.gelu(h).astype(jnp.bfloat16) for h in halves_dot(slot_in, w_in_ref)], axis=1)
    out = jnp.concatenate([o.astype(jnp.bfloat16) for o in halves_dot(hidden, w_out_ref)], axis=1)
    for k in range(devices):
        out_ref[k] = out


def expert(got, w_in, w_out):
    devices, slots, _ = got.shape
    return pl.pallas_call(
        expert_kernel,
        out_shape=jax.ShapeDtypeStruct((devices, slots, w_in.shape[1]), jnp.bfloat16),
        in_specs=[pl.BlockSpec(memory_space=pltpu.VMEM)] * 3,
        out_specs=pl.BlockSpec(memory_space=pltpu.VMEM),
        compiler_params=pltpu.CompilerParams(vmem_limit_bytes=16 * MIB),
        cost_estimate=pl.CostEstimate(flops=4 * slots * w_in.size, bytes_accessed=4 * w_in.size, transcendentals=slots * w_in.shape[2]),
        name="expert",
    )(got, *(pltpu.with_memory_space_constraint(w, pltpu.VMEM) for w in (w_in, w_out)))


def mix_kernel(chunks, logits_ref, slot_ref, mixed_ref, slot_all, held, sem):
    for k in range(slot_ref.shape[0]):
        slot_all[SLOTS * ORDER2[k] : SLOTS * (ORDER2[k] + 1), :] = slot_ref[k]
    starts = [sum(chunks[:i]) for i in range(len(chunks))]

    def copy(i):
        part = pl.ds(starts[i], chunks[i])
        return pltpu.make_async_copy(held.at[part], mixed_ref.at[part], sem.at[i])

    for i in range(len(chunks)):
        rows = chunks[i] // 2
        for part in [pl.ds(starts[i] + k * rows, rows) for k in range(2)]:
            block = logits_ref[part, :]
            shifted = jnp.exp(block - jnp.max(block, axis=1, keepdims=True))
            combine = (shifted / jnp.sum(shifted, axis=1, keepdims=True)).astype(jnp.bfloat16)
            held[part, :] = jnp.dot(combine, slot_all[...], preferred_element_type=jnp.float32).astype(jnp.bfloat16)
        copy(i).start()
    for i in range(len(chunks)):
        copy(i).wait()


def mix(logits, slot_all):
    count, slots = logits.shape
    width = slot_all.shape[2]
    chunks = (count // 8,) * 8
    return pl.pallas_call(
        functools.partial(mix_kernel, chunks),
        out_shape=jax.ShapeDtypeStruct((count, width), jnp.bfloat16),
        in_specs=[pl.BlockSpec(memory_space=pltpu.VMEM)] * 2,
        out_specs=pl.BlockSpec(memory_space=pl.ANY),
        scratch_shapes=[
            pltpu.VMEM((slots, width), jnp.bfloat16),
            pltpu.VMEM((count, width), jnp.bfloat16),
            pltpu.SemaphoreType.DMA((len(chunks),)),
        ],
        compiler_params=pltpu.CompilerParams(vmem_limit_bytes=24 * MIB),
        cost_estimate=pl.CostEstimate(flops=2 * count * width * slots, bytes_accessed=2 * count * width, transcendentals=count * slots),
        name="mix",
    )(logits, slot_all)


def body(tokens, slot_proj, w_in, w_out):
    devices = lax.axis_size("seq")
    sent, logits = dispatch(tokens, slot_proj, devices)
    got = lax.all_to_all(sent, "seq", 0, 0, axis_index_groups=[list(ORDER1)])
    slot_out = expert(got, w_in, w_out)
    slot_all = lax.all_to_all(slot_out, "seq", 0, 0, axis_index_groups=[list(ORDER2)])
    return mix(logits, slot_all)


def solution(mesh):
    return jax.shard_map(
        body,
        mesh=mesh,
        in_specs=(P(("clip", "seq"), None), P(), P("seq", None, None), P("seq", None, None)),
        out_specs=P(("clip", "seq"), None),
        check_vma=False,
    )
```

```python
import functools

import jax
import jax.numpy as jnp
from jax import lax
from jax.experimental import pallas as pl
from jax.experimental.pallas import tpu as pltpu
from jax.sharding import PartitionSpec as P

SLOTS = 2
LANES = 128
MIB = 1 << 20
SIDE = 4


def steps_from_origin(index):
    x, z = index // (2 * SIDE), index // 2 % SIDE
    return min(x, SIDE - x) + min(z, SIDE - z)


ORDER1 = [(23 - i) % 32 for i in range(32)]
ORDER2 = sorted(range(32), key=lambda i: (steps_from_origin(i), i), reverse=True)


def split3(x):
    hi = x.astype(jnp.bfloat16).astype(jnp.float32)
    mid = (x - hi).astype(jnp.bfloat16).astype(jnp.float32)
    return [hi, mid, x - hi - mid]


def dispatch_kernel(chunks, tokens_ref, proj_hbm, sent_ref, logits_ref, held, acc, proj_ref, sem):
    slots, width = proj_ref.shape
    starts = [sum(chunks[:i]) for i in range(len(chunks))]

    def copy(i):
        part = pl.ds(starts[i], chunks[i])
        return pltpu.make_async_copy(tokens_ref.at[part], held.at[part], sem.at[i])

    proj_copy = pltpu.make_async_copy(proj_hbm, proj_ref, sem.at[len(chunks)])
    copy(0).start()
    proj_copy.start()
    for i in range(1, len(chunks)):
        copy(i).start()
    proj_copy.wait()

    def halves(i):
        rows = chunks[i] // 2
        return [pl.ds(starts[i] + k * rows, rows) for k in range(2)]

    def chunk_logits(i):
        copy(i).wait()
        blocks = []
        for part in halves(i):
            block = lax.dot_general(
                held[part, :], proj_ref[...], (((1,), (1,)), ((), ())), preferred_element_type=jnp.float32
            )
            logits_ref[part, :] = block
            blocks.append(block)
        return blocks

    top = jnp.full((1, slots), -jnp.inf, jnp.float32)
    total = jnp.zeros((1, slots), jnp.float32)
    blocks = chunk_logits(0)
    for i in range(len(chunks)):
        following = chunk_logits(i + 1) if i + 1 < len(chunks) else None
        new_top = top
        for block in blocks:
            new_top = jnp.maximum(new_top, jnp.max(block, axis=0, keepdims=True))
        fade = jnp.exp(top - new_top)
        total = total * fade
        adds = []
        for part, block in zip(halves(i), blocks):
            shifted = jnp.exp(block - new_top)
            total = total + jnp.sum(shifted, axis=0, keepdims=True)
            adds.append(
                lax.dot_general(
                    shifted.astype(jnp.bfloat16), held[part, :], (((0,), (0,)), ((), ())),
                    preferred_element_type=jnp.float32,
                )
            )
        add = adds[0] + adds[1]
        acc[...] = add if i == 0 else acc[...] * fade.reshape(slots, 1) + add
        top, blocks = new_top, following
    lanes = [*split3(top), *split3(total)]
    stats = jnp.concatenate([*lanes, jnp.zeros((LANES - len(lanes), slots), jnp.float32)], axis=0)
    sums = acc[...].astype(jnp.bfloat16)
    stats = stats.T.astype(jnp.bfloat16)
    for j in range(slots // SLOTS):
        k = ORDER1[j]
        sent_ref[j, :, :width] = sums[SLOTS * k : SLOTS * (k + 1), :]
        sent_ref[j, :, width:] = stats[SLOTS * k : SLOTS * (k + 1), :]


def dispatch(tokens, slot_proj, devices):
    count, width = tokens.shape
    slots = slot_proj.shape[1]
    unit = count // 20
    chunks = (3 * unit, 4 * unit, 6 * unit, 7 * unit)
    return pl.pallas_call(
        functools.partial(dispatch_kernel, chunks),
        out_shape=(
            jax.ShapeDtypeStruct((devices, slots // devices, width + LANES), jnp.bfloat16),
            jax.ShapeDtypeStruct((count, slots), jnp.float32),
        ),
        in_specs=[pl.BlockSpec(memory_space=pltpu.HBM)] * 2,
        out_specs=(pl.BlockSpec(memory_space=pltpu.VMEM), pl.BlockSpec(memory_space=pltpu.VMEM)),
        scratch_shapes=[
            pltpu.VMEM((count, width), jnp.bfloat16),
            pltpu.VMEM((slots, width), jnp.float32),
            pltpu.VMEM((slots, width), jnp.bfloat16),
            pltpu.SemaphoreType.DMA((len(chunks) + 1,)),
        ],
        compiler_params=pltpu.CompilerParams(vmem_limit_bytes=20 * MIB),
        cost_estimate=pl.CostEstimate(
            flops=32 * count * width * slots, bytes_accessed=2 * count * width, transcendentals=count * slots
        ),
        name="dispatch",
    )(pltpu.with_memory_space_constraint(tokens, pltpu.HBM), pltpu.with_memory_space_constraint(slot_proj.T, pltpu.HBM))


def halves_dot(rows, weights_ref):
    half = weights_ref.shape[2] // 2
    return [
        jnp.dot(rows, weights_ref[0, :, k * half : (k + 1) * half], preferred_element_type=jnp.float32) for k in range(2)
    ]


def expert_kernel(got_ref, w_in_ref, w_out_ref, out_ref):
    width = w_in_ref.shape[1]
    devices = got_ref.shape[0]
    stats = got_ref[:, :, width:].astype(jnp.float32)
    maxes = stats[:, :, 0:1] + stats[:, :, 1:2] + stats[:, :, 2:3]
    totals = stats[:, :, 3:4] + stats[:, :, 4:5] + stats[:, :, 5:6]
    scale = jnp.exp(maxes - jnp.max(maxes, axis=0, keepdims=True))
    terms = [got_ref[k, :, :width].astype(jnp.float32) * scale[k] for k in range(devices)]
    while len(terms) > 4:
        terms = [sum(terms[k + 4 :: 4], terms[k]) for k in range(4)]
    num = (terms[0] + terms[1]) + (terms[2] + terms[3])
    slot_in = (num / jnp.sum(totals * scale, axis=0)).astype(jnp.bfloat16)
    hidden = jnp.concatenate([jax.nn.gelu(h).astype(jnp.bfloat16) for h in halves_dot(slot_in, w_in_ref)], axis=1)
    out = jnp.concatenate([o.astype(jnp.bfloat16) for o in halves_dot(hidden, w_out_ref)], axis=1)
    for k in range(devices):
        out_ref[k] = out


def expert(got, w_in, w_out):
    devices, slots, _ = got.shape
    return pl.pallas_call(
        expert_kernel,
        out_shape=jax.ShapeDtypeStruct((devices, slots, w_in.shape[1]), jnp.bfloat16),
        in_specs=[pl.BlockSpec(memory_space=pltpu.VMEM)] * 3,
        out_specs=pl.BlockSpec(memory_space=pltpu.VMEM),
        compiler_params=pltpu.CompilerParams(vmem_limit_bytes=16 * MIB),
        cost_estimate=pl.CostEstimate(flops=4 * slots * w_in.size, bytes_accessed=4 * w_in.size, transcendentals=slots * w_in.shape[2]),
        name="expert",
    )(got, *(pltpu.with_memory_space_constraint(w, pltpu.VMEM) for w in (w_in, w_out)))


def mix_kernel(chunks, logits_ref, slot_ref, mixed_ref, slot_all, held, sem):
    for k in range(slot_ref.shape[0]):
        slot_all[SLOTS * ORDER2[k] : SLOTS * (ORDER2[k] + 1), :] = slot_ref[k]
    starts = [sum(chunks[:i]) for i in range(len(chunks))]

    def copy(i):
        part = pl.ds(starts[i], chunks[i])
        return pltpu.make_async_copy(held.at[part], mixed_ref.at[part], sem.at[i])

    for i in range(len(chunks)):
        rows = chunks[i] // 2
        for part in [pl.ds(starts[i] + k * rows, rows) for k in range(2)]:
            block = logits_ref[part, :]
            shifted = jnp.exp(block - jnp.max(block, axis=1, keepdims=True))
            combine = (shifted / jnp.sum(shifted, axis=1, keepdims=True)).astype(jnp.bfloat16)
            held[part, :] = jnp.dot(combine, slot_all[...], preferred_element_type=jnp.float32).astype(jnp.bfloat16)
        copy(i).start()
    for i in range(len(chunks)):
        copy(i).wait()


def mix(logits, slot_all):
    count, slots = logits.shape
    width = slot_all.shape[2]
    chunks = (count // 8,) * 8
    return pl.pallas_call(
        functools.partial(mix_kernel, chunks),
        out_shape=jax.ShapeDtypeStruct((count, width), jnp.bfloat16),
        in_specs=[pl.BlockSpec(memory_space=pltpu.VMEM)] * 2,
        out_specs=pl.BlockSpec(memory_space=pl.ANY),
        scratch_shapes=[
            pltpu.VMEM((slots, width), jnp.bfloat16),
            pltpu.VMEM((count, width), jnp.bfloat16),
            pltpu.SemaphoreType.DMA((len(chunks),)),
        ],
        compiler_params=pltpu.CompilerParams(vmem_limit_bytes=24 * MIB),
        cost_estimate=pl.CostEstimate(flops=2 * count * width * slots, bytes_accessed=2 * count * width, transcendentals=count * slots),
        name="mix",
    )(logits, slot_all)


def body(tokens, slot_proj, w_in, w_out):
    devices = lax.axis_size("seq")
    sent, logits = dispatch(tokens, slot_proj, devices)
    got = lax.all_to_all(sent, "seq", 0, 0, axis_index_groups=[list(ORDER1)])
    slot_out = expert(got, w_in, w_out)
    slot_all = lax.all_to_all(slot_out, "seq", 0, 0, axis_index_groups=[list(ORDER2)])
    return mix(logits, slot_all)


def solution(mesh):
    return jax.shard_map(
        body,
        mesh=mesh,
        in_specs=(P(("clip", "seq"), None), P(), P("seq", None, None), P("seq", None, None)),
        out_specs=P(("clip", "seq"), None),
        check_vma=False,
    )
```

```python
import functools

import jax
import jax.numpy as jnp
from jax import lax
from jax.experimental import pallas as pl
from jax.experimental.pallas import tpu as pltpu
from jax.sharding import PartitionSpec as P

SLOTS = 2
LANES = 128
MIB = 1 << 20
SIDE = 4


def steps_from_origin(index):
    x, z = index // (2 * SIDE), index // 2 % SIDE
    return min(x, SIDE - x) + min(z, SIDE - z)


ORDER1 = [(23 - i) % 32 for i in range(32)]
ORDER2 = sorted(range(32), key=lambda i: (steps_from_origin(i), i), reverse=True)


def split3(x):
    hi = x.astype(jnp.bfloat16).astype(jnp.float32)
    mid = (x - hi).astype(jnp.bfloat16).astype(jnp.float32)
    return [hi, mid, x - hi - mid]


def dispatch_kernel(chunks, tokens_ref, proj_hbm, sent_ref, logits_ref, held, acc, proj_ref, sem):
    slots, width = proj_ref.shape
    starts = [sum(chunks[:i]) for i in range(len(chunks))]

    def copy(i):
        part = pl.ds(starts[i], chunks[i])
        return pltpu.make_async_copy(tokens_ref.at[part], held.at[part], sem.at[i])

    proj_copy = pltpu.make_async_copy(proj_hbm, proj_ref, sem.at[len(chunks)])
    copy(0).start()
    proj_copy.start()
    for i in range(1, len(chunks)):
        copy(i).start()
    proj_copy.wait()

    def halves(i):
        rows = chunks[i] // 2
        return [pl.ds(starts[i] + k * rows, rows) for k in range(2)]

    def chunk_logits(i):
        copy(i).wait()
        blocks = []
        for part in halves(i):
            block = lax.dot_general(
                held[part, :], proj_ref[...], (((1,), (1,)), ((), ())), preferred_element_type=jnp.float32
            )
            logits_ref[part, :] = block
            blocks.append(block)
        return blocks

    top = jnp.full((1, slots), -jnp.inf, jnp.float32)
    total = jnp.zeros((1, slots), jnp.float32)
    blocks = chunk_logits(0)
    for i in range(len(chunks)):
        following = chunk_logits(i + 1) if i + 1 < len(chunks) else None
        new_top = top
        for block in blocks:
            new_top = jnp.maximum(new_top, jnp.max(block, axis=0, keepdims=True))
        fade = jnp.exp(top - new_top)
        total = total * fade
        weights = []
        for block in blocks:
            shifted = jnp.exp(block - new_top)
            total = total + jnp.sum(shifted, axis=0, keepdims=True)
            weights.append(shifted.astype(jnp.bfloat16))
        weights = jnp.concatenate(weights, axis=0)
        kept = fade.reshape(slots, 1)
        cut = width * 3 // 5
        for columns in (slice(0, cut), slice(cut, width)):
            add = lax.dot_general(
                weights, held[pl.ds(starts[i], chunks[i]), columns], (((0,), (0,)), ((), ())),
                preferred_element_type=jnp.float32,
            )
            acc[:, columns] = add if i == 0 else acc[:, columns] * kept + add
        top, blocks = new_top, following
    lanes = [*split3(top), *split3(total)]
    stats = jnp.concatenate([*lanes, jnp.zeros((LANES - len(lanes), slots), jnp.float32)], axis=0)
    sums = acc[...].astype(jnp.bfloat16)
    stats = stats.T.astype(jnp.bfloat16)
    for j in range(slots // SLOTS):
        k = ORDER1[j]
        sent_ref[j, :, :width] = sums[SLOTS * k : SLOTS * (k + 1), :]
        sent_ref[j, :, width:] = stats[SLOTS * k : SLOTS * (k + 1), :]


def dispatch(tokens, slot_proj, devices):
    count, width = tokens.shape
    slots = slot_proj.shape[1]
    unit = count // 20
    chunks = (3 * unit, 4 * unit, 6 * unit, 7 * unit)
    return pl.pallas_call(
        functools.partial(dispatch_kernel, chunks),
        out_shape=(
            jax.ShapeDtypeStruct((devices, slots // devices, width + LANES), jnp.bfloat16),
            jax.ShapeDtypeStruct((count, slots), jnp.float32),
        ),
        in_specs=[pl.BlockSpec(memory_space=pltpu.HBM)] * 2,
        out_specs=(pl.BlockSpec(memory_space=pltpu.VMEM), pl.BlockSpec(memory_space=pltpu.VMEM)),
        scratch_shapes=[
            pltpu.VMEM((count, width), jnp.bfloat16),
            pltpu.VMEM((slots, width), jnp.float32),
            pltpu.VMEM((slots, width), jnp.bfloat16),
            pltpu.SemaphoreType.DMA((len(chunks) + 1,)),
        ],
        compiler_params=pltpu.CompilerParams(vmem_limit_bytes=20 * MIB),
        cost_estimate=pl.CostEstimate(
            flops=32 * count * width * slots, bytes_accessed=2 * count * width, transcendentals=count * slots
        ),
        name="dispatch",
    )(pltpu.with_memory_space_constraint(tokens, pltpu.HBM), pltpu.with_memory_space_constraint(slot_proj.T, pltpu.HBM))


def halves_dot(rows, weights_ref):
    half = weights_ref.shape[2] // 2
    return [
        jnp.dot(rows, weights_ref[0, :, k * half : (k + 1) * half], preferred_element_type=jnp.float32) for k in range(2)
    ]


def expert_kernel(got_ref, w_in_ref, w_out_ref, out_ref):
    width = w_in_ref.shape[1]
    devices = got_ref.shape[0]
    stats = got_ref[:, :, width:].astype(jnp.float32)
    maxes = stats[:, :, 0:1] + stats[:, :, 1:2] + stats[:, :, 2:3]
    totals = stats[:, :, 3:4] + stats[:, :, 4:5] + stats[:, :, 5:6]
    scale = jnp.exp(maxes - jnp.max(maxes, axis=0, keepdims=True))
    terms = [got_ref[k, :, :width].astype(jnp.float32) * scale[k] for k in range(devices)]
    while len(terms) > 4:
        terms = [sum(terms[k + 4 :: 4], terms[k]) for k in range(4)]
    num = (terms[0] + terms[1]) + (terms[2] + terms[3])
    slot_in = (num / jnp.sum(totals * scale, axis=0)).astype(jnp.bfloat16)
    hidden = jnp.concatenate([jax.nn.gelu(h).astype(jnp.bfloat16) for h in halves_dot(slot_in, w_in_ref)], axis=1)
    out = jnp.concatenate([o.astype(jnp.bfloat16) for o in halves_dot(hidden, w_out_ref)], axis=1)
    for k in range(devices):
        out_ref[k] = out


def expert(got, w_in, w_out):
    devices, slots, _ = got.shape
    return pl.pallas_call(
        expert_kernel,
        out_shape=jax.ShapeDtypeStruct((devices, slots, w_in.shape[1]), jnp.bfloat16),
        in_specs=[pl.BlockSpec(memory_space=pltpu.VMEM)] * 3,
        out_specs=pl.BlockSpec(memory_space=pltpu.VMEM),
        compiler_params=pltpu.CompilerParams(vmem_limit_bytes=16 * MIB),
        cost_estimate=pl.CostEstimate(flops=4 * slots * w_in.size, bytes_accessed=4 * w_in.size, transcendentals=slots * w_in.shape[2]),
        name="expert",
    )(got, *(pltpu.with_memory_space_constraint(w, pltpu.VMEM) for w in (w_in, w_out)))


def mix_kernel(chunks, logits_ref, slot_ref, mixed_ref, slot_all, held, sem):
    for k in range(slot_ref.shape[0]):
        slot_all[SLOTS * ORDER2[k] : SLOTS * (ORDER2[k] + 1), :] = slot_ref[k]
    starts = [sum(chunks[:i]) for i in range(len(chunks))]

    def copy(i):
        part = pl.ds(starts[i], chunks[i])
        return pltpu.make_async_copy(held.at[part], mixed_ref.at[part], sem.at[i])

    for i in range(len(chunks)):
        rows = chunks[i] // 2
        for part in [pl.ds(starts[i] + k * rows, rows) for k in range(2)]:
            block = logits_ref[part, :]
            shifted = jnp.exp(block - jnp.max(block, axis=1, keepdims=True))
            combine = (shifted / jnp.sum(shifted, axis=1, keepdims=True)).astype(jnp.bfloat16)
            held[part, :] = jnp.dot(combine, slot_all[...], preferred_element_type=jnp.float32).astype(jnp.bfloat16)
        copy(i).start()
    for i in range(len(chunks)):
        copy(i).wait()


def mix(logits, slot_all):
    count, slots = logits.shape
    width = slot_all.shape[2]
    chunks = (count // 8,) * 8
    return pl.pallas_call(
        functools.partial(mix_kernel, chunks),
        out_shape=jax.ShapeDtypeStruct((count, width), jnp.bfloat16),
        in_specs=[pl.BlockSpec(memory_space=pltpu.VMEM)] * 2,
        out_specs=pl.BlockSpec(memory_space=pl.ANY),
        scratch_shapes=[
            pltpu.VMEM((slots, width), jnp.bfloat16),
            pltpu.VMEM((count, width), jnp.bfloat16),
            pltpu.SemaphoreType.DMA((len(chunks),)),
        ],
        compiler_params=pltpu.CompilerParams(vmem_limit_bytes=24 * MIB),
        cost_estimate=pl.CostEstimate(flops=2 * count * width * slots, bytes_accessed=2 * count * width, transcendentals=count * slots),
        name="mix",
    )(logits, slot_all)


def body(tokens, slot_proj, w_in, w_out):
    devices = lax.axis_size("seq")
    sent, logits = dispatch(tokens, slot_proj, devices)
    got = lax.all_to_all(sent, "seq", 0, 0, axis_index_groups=[list(ORDER1)])
    slot_out = expert(got, w_in, w_out)
    slot_all = lax.all_to_all(slot_out, "seq", 0, 0, axis_index_groups=[list(ORDER2)])
    return mix(logits, slot_all)


def solution(mesh):
    return jax.shard_map(
        body,
        mesh=mesh,
        in_specs=(P(("clip", "seq"), None), P(), P("seq", None, None), P("seq", None, None)),
        out_specs=P(("clip", "seq"), None),
        check_vma=False,
    )
```

```python
import functools

import jax
import jax.numpy as jnp
from jax import lax
from jax.experimental import pallas as pl
from jax.experimental.pallas import tpu as pltpu
from jax.sharding import PartitionSpec as P

SLOTS = 2
LANES = 128
MIB = 1 << 20
SIDE = 4


def steps_from_origin(index):
    x, z = index // (2 * SIDE), index // 2 % SIDE
    return min(x, SIDE - x) + min(z, SIDE - z)


ORDER1 = [(23 - i) % 32 for i in range(32)]
ORDER2 = sorted(range(32), key=lambda i: (steps_from_origin(i), i), reverse=True)


def split3(x):
    hi = x.astype(jnp.bfloat16).astype(jnp.float32)
    mid = (x - hi).astype(jnp.bfloat16).astype(jnp.float32)
    return [hi, mid, x - hi - mid]


def dispatch_kernel(chunks, tokens_ref, proj_hbm, sent_ref, logits_ref, held, acc, proj_ref, sem):
    slots, width = proj_ref.shape
    starts = [sum(chunks[:i]) for i in range(len(chunks))]

    def copy(i):
        part = pl.ds(starts[i], chunks[i])
        return pltpu.make_async_copy(tokens_ref.at[part], held.at[part], sem.at[i])

    proj_copy = pltpu.make_async_copy(proj_hbm, proj_ref, sem.at[len(chunks)])
    copy(0).start()
    proj_copy.start()
    for i in range(1, len(chunks)):
        copy(i).start()
    proj_copy.wait()

    def halves(i):
        rows = chunks[i] // 2
        return [pl.ds(starts[i] + k * rows, rows) for k in range(2)]

    def chunk_logits(i):
        copy(i).wait()
        blocks = []
        for part in halves(i):
            block = lax.dot_general(
                held[part, :], proj_ref[...], (((1,), (1,)), ((), ())), preferred_element_type=jnp.float32
            )
            logits_ref[part, :] = block
            blocks.append(block)
        return blocks

    top = jnp.full((1, slots), -jnp.inf, jnp.float32)
    total = jnp.zeros((1, slots), jnp.float32)
    blocks = chunk_logits(0)
    for i in range(len(chunks)):
        following = chunk_logits(i + 1) if i + 1 < len(chunks) else None
        new_top = top
        for block in blocks:
            new_top = jnp.maximum(new_top, jnp.max(block, axis=0, keepdims=True))
        fade = jnp.exp(top - new_top)
        total = total * fade
        adds = []
        for part, block in zip(halves(i), blocks):
            shifted = jnp.exp(block - new_top)
            total = total + jnp.sum(shifted, axis=0, keepdims=True)
            adds.append(
                lax.dot_general(
                    shifted.astype(jnp.bfloat16), held[part, :], (((0,), (0,)), ((), ())),
                    preferred_element_type=jnp.float32,
                )
            )
        add = adds[0] + adds[1]
        acc[...] = add if i == 0 else acc[...] * fade.reshape(slots, 1) + add
        top, blocks = new_top, following
    lanes = [*split3(top), *split3(total)]
    stats = jnp.concatenate([*lanes, jnp.zeros((LANES - len(lanes), slots), jnp.float32)], axis=0)
    sums = acc[...].astype(jnp.bfloat16)
    stats = stats.T.astype(jnp.bfloat16)
    for j in range(slots // SLOTS):
        k = ORDER1[j]
        sent_ref[j, :, :width] = sums[SLOTS * k : SLOTS * (k + 1), :]
        sent_ref[j, :, width:] = stats[SLOTS * k : SLOTS * (k + 1), :]


def dispatch(tokens, slot_proj, devices):
    count, width = tokens.shape
    slots = slot_proj.shape[1]
    unit = count // 20
    chunks = (3 * unit, 4 * unit, 6 * unit, 7 * unit)
    return pl.pallas_call(
        functools.partial(dispatch_kernel, chunks),
        out_shape=(
            jax.ShapeDtypeStruct((devices, slots // devices, width + LANES), jnp.bfloat16),
            jax.ShapeDtypeStruct((count, slots), jnp.float32),
        ),
        in_specs=[pl.BlockSpec(memory_space=pltpu.HBM)] * 2,
        out_specs=(pl.BlockSpec(memory_space=pltpu.VMEM), pl.BlockSpec(memory_space=pltpu.VMEM)),
        scratch_shapes=[
            pltpu.VMEM((count, width), jnp.bfloat16),
            pltpu.VMEM((slots, width), jnp.float32),
            pltpu.VMEM((slots, width), jnp.bfloat16),
            pltpu.SemaphoreType.DMA((len(chunks) + 1,)),
        ],
        compiler_params=pltpu.CompilerParams(vmem_limit_bytes=20 * MIB),
        cost_estimate=pl.CostEstimate(
            flops=32 * count * width * slots, bytes_accessed=2 * count * width, transcendentals=count * slots
        ),
        name="dispatch",
    )(pltpu.with_memory_space_constraint(tokens, pltpu.HBM), pltpu.with_memory_space_constraint(slot_proj.T, pltpu.HBM))


def halves_dot(rows, weights_ref):
    half = weights_ref.shape[2] // 2
    return [
        jnp.dot(rows, weights_ref[0, :, k * half : (k + 1) * half], preferred_element_type=jnp.float32) for k in range(2)
    ]


def expert_kernel(got_ref, w_in_ref, w_out_ref, out_ref):
    width = w_in_ref.shape[1]
    devices = got_ref.shape[0]
    stats = got_ref[:, :, width:].astype(jnp.float32)
    maxes = stats[:, :, 0:1] + stats[:, :, 1:2] + stats[:, :, 2:3]
    totals = stats[:, :, 3:4] + stats[:, :, 4:5] + stats[:, :, 5:6]
    scale = jnp.exp(maxes - jnp.max(maxes, axis=0, keepdims=True))
    terms = [got_ref[k, :, :width].astype(jnp.float32) * scale[k] for k in range(devices)]
    while len(terms) > 4:
        terms = [sum(terms[k + 4 :: 4], terms[k]) for k in range(4)]
    num = (terms[0] + terms[1]) + (terms[2] + terms[3])
    slot_in = (num / jnp.sum(totals * scale, axis=0)).astype(jnp.bfloat16)
    hidden = jnp.concatenate([jax.nn.gelu(h).astype(jnp.bfloat16) for h in halves_dot(slot_in, w_in_ref)], axis=1)
    out = jnp.concatenate([o.astype(jnp.bfloat16) for o in halves_dot(hidden, w_out_ref)], axis=1)
    for k in range(devices):
        out_ref[k] = out


def expert(got, w_in, w_out):
    devices, slots, _ = got.shape
    return pl.pallas_call(
        expert_kernel,
        out_shape=jax.ShapeDtypeStruct((devices, slots, w_in.shape[1]), jnp.bfloat16),
        in_specs=[pl.BlockSpec(memory_space=pltpu.VMEM)] * 3,
        out_specs=pl.BlockSpec(memory_space=pltpu.VMEM),
        compiler_params=pltpu.CompilerParams(vmem_limit_bytes=16 * MIB),
        cost_estimate=pl.CostEstimate(flops=4 * slots * w_in.size, bytes_accessed=4 * w_in.size, transcendentals=slots * w_in.shape[2]),
        name="expert",
    )(got, *(pltpu.with_memory_space_constraint(w, pltpu.VMEM) for w in (w_in, w_out)))


def mix_kernel(chunks, logits_ref, slot_ref, mixed_ref, slot_all, held, sem):
    for k in range(slot_ref.shape[0]):
        slot_all[SLOTS * ORDER2[k] : SLOTS * (ORDER2[k] + 1), :] = slot_ref[k]
    starts = [sum(chunks[:i]) for i in range(len(chunks))]

    def copy(i):
        part = pl.ds(starts[i], chunks[i])
        return pltpu.make_async_copy(held.at[part], mixed_ref.at[part], sem.at[i])

    for i in range(len(chunks)):
        rows = chunks[i] // 2
        for part in [pl.ds(starts[i] + k * rows, rows) for k in range(2)]:
            block = logits_ref[part, :]
            shifted = jnp.exp(block - jnp.max(block, axis=1, keepdims=True))
            combine = (shifted * (1.0 / jnp.sum(shifted, axis=1, keepdims=True))).astype(jnp.bfloat16)
            held[part, :] = jnp.dot(combine, slot_all[...], preferred_element_type=jnp.float32).astype(jnp.bfloat16)
        copy(i).start()
    for i in range(len(chunks)):
        copy(i).wait()


def mix(logits, slot_all):
    count, slots = logits.shape
    width = slot_all.shape[2]
    chunks = (count // 8,) * 8
    return pl.pallas_call(
        functools.partial(mix_kernel, chunks),
        out_shape=jax.ShapeDtypeStruct((count, width), jnp.bfloat16),
        in_specs=[pl.BlockSpec(memory_space=pltpu.VMEM)] * 2,
        out_specs=pl.BlockSpec(memory_space=pl.ANY),
        scratch_shapes=[
            pltpu.VMEM((slots, width), jnp.bfloat16),
            pltpu.VMEM((count, width), jnp.bfloat16),
            pltpu.SemaphoreType.DMA((len(chunks),)),
        ],
        compiler_params=pltpu.CompilerParams(vmem_limit_bytes=24 * MIB),
        cost_estimate=pl.CostEstimate(flops=2 * count * width * slots, bytes_accessed=2 * count * width, transcendentals=count * slots),
        name="mix",
    )(logits, slot_all)


def body(tokens, slot_proj, w_in, w_out):
    devices = lax.axis_size("seq")
    sent, logits = dispatch(tokens, slot_proj, devices)
    got = lax.all_to_all(sent, "seq", 0, 0, axis_index_groups=[list(ORDER1)])
    slot_out = expert(got, w_in, w_out)
    slot_all = lax.all_to_all(slot_out, "seq", 0, 0, axis_index_groups=[list(ORDER2)])
    return mix(logits, slot_all)


def solution(mesh):
    return jax.shard_map(
        body,
        mesh=mesh,
        in_specs=(P(("clip", "seq"), None), P(), P("seq", None, None), P("seq", None, None)),
        out_specs=P(("clip", "seq"), None),
        check_vma=False,
    )
```
